512 devices in a mesh: row: 32 (over y_hi, z), col: 16 (over y_lo, x, core).
Axes of the slice: x: 4, y: 4 (y_hi: 2, y_lo: 2; y = y_hi * 2 + y_lo), z: 16, core: 2. Of those that a mesh axis runs over, the one named last changes fastest.
Arguments:
- features: bfloat16 [16, 1024, 256], P('col', 'row'), may hold values from -6 to 6
- node_order: int32 [16, 1024], P('col'), may hold values from 0 to 1023, each once within a row
- tile_weights: bfloat16 [16384, 128, 128], P(('row', 'col')), may hold values from 0 to 4, as said below
- tile_rows: int32 [16384], P(('row', 'col')), may hold values from 0 to 7, as said below
- tile_cols: int32 [16384], P(('row', 'col')), may hold values from 0 to 7
- tile_count: int32 [512], P(('row', 'col')), may hold values from 8 to 32, as said below
- weight: bfloat16 [256, 256], replicated, may hold values from -0.375 to 0.375
- bias_vector: float32 [256], replicated, may hold values from -3 to 3
- cotangent: bfloat16 [32768, 256], P(('row', 'col')), may hold values from -6 to 6
Outputs:
- output: bfloat16 [32768, 256], P(('row', 'col'))
- feature_grad: bfloat16 [16, 1024, 256], P('col', 'row')
- weight_grad: float32 [256, 256], replicated
- bias_grad: float32 [256], replicated
The draws below stay inside these ranges and needn't reach their ends.
Inputs may be any that keep to these rules, and one draw needn't show every extreme that they name: Device block b (row index times 16 plus column index) uses slots 0 to tile_count[b] - 1 of its 32; later slots are ignored. At least one device uses all 32 slots. `tile_weights`: every entry is a whole number. `tile_rows`: in a row block, up to two of its 8 destination tiles (never all) may be named by no slot of any of its devices; at least one row block leaves one or more tiles out.
All inputs are finite; a program needn't handle non-finite values.
Results may differ from the reference program's by a relative error of at most 0.0075.
Values may be sent and summed in bfloat16 or wider, within the bound.
No kernel may reach another device: no remote copies, remote signals or barrier semaphores. Data moves between devices by JAX's collectives and lax.ppermute only.
A program may use at most 64 MiB of HBM per device.

```python
import jax
import jax.numpy as jnp
from jax import lax

F = 256
TILE = 128
DEST_TILES = 8
ST = 8
K = 32
SB = 1024
NDST = 32768
N_ROW = 32
N_COL = 16


def draw_tile_count(key, part):
    key = jax.random.fold_in(key, 7)
    devices = N_ROW * N_COL
    shifts = jax.random.randint(key, (devices,), 0, 8)
    floor_count = max(K // 4, 1)
    counts = jnp.maximum(jnp.right_shift(jnp.full((devices,), K, jnp.int32), shifts), floor_count)
    full_at = jax.random.randint(jax.random.fold_in(key, 1), (), 0, devices)
    return counts.at[full_at].set(K).astype(jnp.int32)


def draw_tile_weights(key, part):
    key = jax.random.fold_in(key, 5)
    levels = jax.random.randint(key, (N_ROW * N_COL * K, TILE, TILE), 0, 128)
    values = jnp.where(levels < 4, levels + 1, 0).astype(jnp.float32)
    return values.astype(jnp.bfloat16)


def reordered_tiles(one_key):
    return jax.random.permutation(one_key, DEST_TILES).astype(jnp.int32)


def draw_tile_rows(key, part):
    key = jax.random.fold_in(key, 11)
    order_keys = jax.random.split(jax.random.fold_in(key, 1), N_ROW)
    orders = jax.vmap(reordered_tiles)(order_keys)
    empty_slots = jax.random.randint(jax.random.fold_in(key, 2), (N_ROW,), 0, 3)
    forced_choice = jax.random.randint(jax.random.fold_in(key, 3), (), 0, N_ROW)
    empty_slots = empty_slots.at[forced_choice].set(jnp.maximum(empty_slots[forced_choice], 1))
    empty_slots = jnp.minimum(empty_slots, DEST_TILES - 1)
    ranking_index = jnp.arange(DEST_TILES, dtype=jnp.int32)
    rank_weight = 720720 // (ranking_index + 1)
    active_rank = ranking_index[None, :] < (DEST_TILES - empty_slots)[:, None]
    weights = jnp.where(active_rank, rank_weight[None, :], 0)
    bounds = jnp.cumsum(weights, axis=1)
    totals = bounds[:, -1]
    drawn_points = jax.random.randint(jax.random.fold_in(key, 4), (N_ROW, N_COL * K), 0, totals[:, None])
    rank_drawn = jnp.sum((drawn_points[:, :, None] >= bounds[:, None, :]).astype(jnp.int32), axis=2)
    tile_index = jnp.take_along_axis(orders, rank_drawn, axis=1)
    return tile_index.reshape(N_ROW * N_COL * K).astype(jnp.int32)


def plant(result, key, smallest, high):
    spot = [jax.random.randint(jax.random.fold_in(key, axis), (), 0, length) for axis, length in enumerate(result.shape)]
    widest = result.shape.index(max(result.shape))
    beside = spot[:widest] + [(spot[widest] + 1) % result.shape[widest]] + spot[widest + 1:]
    return result.at[tuple(spot)].set(smallest).at[tuple(beside)].set(high)


def shard_levels(own_key, dims, pieces, low, top_value):
    def one(position, shards_of):
        draws = jax.random.uniform(jax.random.fold_in(jax.random.fold_in(own_key, 6), position), (shards_of,), jnp.float32, low / len(pieces), top_value / len(pieces))
        return jnp.repeat(jnp.exp(draws), dims[position] // shards_of).reshape((-1,) + (1,) * (len(dims) - position - 1))

    gain = one(*pieces[0])
    for cut in pieces[1:]:
        gain = gain * one(*cut)
    return gain


def scatter_about(rng, dims, width, reach, cuts=(), held_as=jnp.bfloat16):
    result = width * jax.random.normal(rng, dims, jnp.float32)
    if cuts:
        result = result * shard_levels(rng, dims, cuts, -0.22, 0.18)
    return jnp.clip(result, -reach, reach).astype(held_as)


def setup_inputs(seed: int = 0) -> dict:
    seeds = jax.random.split(jax.random.key(seed), 10)
    features = scatter_about(seeds[0], (N_COL, SB, F), 1.0, 6.0, ((0, 16), (1, 32)))
    node_order = jax.vmap(lambda own: jax.random.permutation(own, SB))(jax.random.split(seeds[1], N_COL)).reshape((N_COL, SB)).astype(jnp.int32)
    tile_weights = draw_tile_weights(jax.random.fold_in(seeds[9], 71), 0)
    tile_rows = draw_tile_rows(jax.random.fold_in(seeds[9], 71), 0)
    tile_cols = plant(jax.random.randint(seeds[4], (N_ROW * N_COL * K,), 0, ST), jax.random.fold_in(seeds[4], 1), 0, ST - 1).astype(jnp.int32)
    tile_count = draw_tile_count(jax.random.fold_in(seeds[9], 71), 0)
    weight = scatter_about(seeds[6], (F, F), F ** -0.5, 0.375)
    bias_vector = scatter_about(seeds[7], (F,), 0.5, 3.0, (), jnp.float32)
    cotangent = scatter_about(seeds[8], (NDST, F), 1.0, 6.0, ((0, 512),))
    return {"features": features, "node_order": node_order, "tile_weights": tile_weights, "tile_rows": tile_rows, "tile_cols": tile_cols, "tile_count": tile_count, "weight": weight, "bias_vector": bias_vector, "cotangent": cotangent}


def permute_rows(block_rows, perm_rows):
    return block_rows[perm_rows]

def restore_rows(block_rows, perm_rows):
    return jnp.zeros_like(block_rows).at[perm_rows].set(block_rows)

def silu_slope(values):
    sigma = jax.nn.sigmoid(values)
    return sigma * (1.0 + values * (1.0 - sigma))

def reference(features, node_order, tile_weights, tile_rows, tile_cols, tile_count, weight, bias_vector, cotangent):
    blocks = N_ROW * N_COL
    ordered = jax.vmap(permute_rows)(features, node_order)
    src_tiles = ordered.reshape(N_COL * ST, TILE, F)
    device_ids = jnp.arange(blocks, dtype=jnp.int32)
    dst_index = (device_ids // N_COL)[:, None] * DEST_TILES + tile_rows.reshape(blocks, K).astype(jnp.int32)
    src_index = (device_ids % N_COL)[:, None] * ST + tile_cols.reshape(blocks, K).astype(jnp.int32)
    weight_blocks = tile_weights.reshape(blocks, K, TILE, TILE)

    def edge_block(weights_blk, count_blk):
        live_slots = jnp.arange(K, dtype=jnp.int32) < count_blk
        return jnp.where(live_slots[:, None, None], weights_blk, jnp.zeros_like(weights_blk)).astype(jnp.float32)

    def forward_block(carry, block_in):
        tile_sums, degree = carry
        weights_blk, rows_blk, cols_blk, count_blk = block_in
        edge_tiles = edge_block(weights_blk, count_blk)
        products = jnp.einsum('kij,kjf->kif', edge_tiles, src_tiles[cols_blk].astype(jnp.float32))
        tile_sums = tile_sums.at[rows_blk].add(products)
        degree = degree.at[rows_blk].add(lax.optimization_barrier(jnp.sum(edge_tiles, axis=2)))
        return ((tile_sums, degree), None)
    start_sums = jnp.zeros((N_ROW * DEST_TILES, TILE, F), jnp.float32)
    start_degree = jnp.zeros((N_ROW * DEST_TILES, TILE), jnp.float32)
    (tile_sums, degree), _ = lax.scan(forward_block, (start_sums, start_degree), (weight_blocks, dst_index, src_index, tile_count))
    row_scale = lax.rsqrt(jnp.maximum(degree.reshape(NDST), 1.0))
    aggregated = (tile_sums.reshape(NDST, F) * row_scale[:, None]).astype(jnp.bfloat16)
    pre_act = jnp.dot(aggregated, weight, preferred_element_type=jnp.float32) + bias_vector
    output = jax.nn.silu(pre_act).astype(jnp.bfloat16)
    grad_pre = (cotangent.astype(jnp.float32) * silu_slope(pre_act)).astype(jnp.bfloat16)
    weight_grad = jnp.dot(aggregated.T, grad_pre, preferred_element_type=jnp.float32)
    bias_grad = lax.optimization_barrier(jnp.sum(grad_pre.astype(jnp.float32), axis=0))
    grad_sums = (jnp.dot(grad_pre, weight.T, preferred_element_type=jnp.float32) * row_scale[:, None]).astype(jnp.bfloat16)
    grad_tiles = grad_sums.reshape(N_ROW * DEST_TILES, TILE, F)

    def backward_block(carry, block_in):
        weights_blk, rows_blk, cols_blk, count_blk = block_in
        edge_tiles = edge_block(weights_blk, count_blk)
        products = jnp.einsum('kij,kif->kjf', edge_tiles, grad_tiles[rows_blk].astype(jnp.float32))
        return (carry.at[cols_blk].add(products), None)
    start_grads = jnp.zeros((N_COL * ST, TILE, F), jnp.float32)
    ordered_grad, _ = lax.scan(backward_block, start_grads, (weight_blocks, dst_index, src_index, tile_count))
    feature_grad = jax.vmap(restore_rows)(ordered_grad.reshape(N_COL, SB, F), node_order).astype(jnp.bfloat16)
    return (output, feature_grad, weight_grad, bias_grad)
```

```python
import jax
import jax.numpy as jnp
from jax import lax
from jax.experimental import pallas as pl
from jax.experimental.pallas import tpu as pltpu
from jax.sharding import PartitionSpec as P

BF16 = jnp.bfloat16
F32 = jnp.float32
NT = (((1,), (1,)), ((), ()))
TN = (((0,), (0,)), ((), ()))
VMEM = pl.BlockSpec(memory_space=pltpu.VMEM)
SMEM = pl.BlockSpec(memory_space=pltpu.SMEM)
PARAMS = pltpu.CompilerParams(vmem_limit_bytes=32 * 1024 * 1024)


def dot_nt(left, right):
    return lax.dot_general(left, right, NT, preferred_element_type=F32)


def edges_kernel(count_ref, rows_ref, cols_ref, order_ref, tiles_ref, m_ref, mt_ref, deg_ref, a_ref, p_ref):
    a_ref[...] = jnp.zeros_like(a_ref)
    tile = tiles_ref.shape[1]

    def add_slot(slot, carry):
        row = pl.multiple_of(rows_ref[slot] * tile, tile)
        col = pl.multiple_of(cols_ref[slot] * tile, tile)
        a_ref[pl.ds(row, tile), pl.ds(col, tile)] += tiles_ref[slot]
        return carry

    lax.fori_loop(0, count_ref[0], add_slot, 0)
    size = a_ref.shape[0]
    order = jnp.broadcast_to(order_ref[...], (size, size))
    places = lax.broadcasted_iota(jnp.int32, (size, size), 0)
    p_ref[...] = jnp.where(places == order, 1.0, 0.0).astype(BF16)
    step = 256
    for start in range(0, size, step):
        part = slice(start, start + step)
        m_ref[:, part] = dot_nt(a_ref[...], p_ref[part, :]).astype(BF16)
        mt_ref[:, part] = dot_nt(p_ref[...], a_ref[part, :]).astype(BF16)
    degree = dot_nt(jnp.ones((16, size), BF16), a_ref[...])
    high = jnp.floor(degree * (1.0 / 128.0))
    deg_ref[:, :size] = high.astype(BF16)
    deg_ref[:, size:] = (degree - 128.0 * high).astype(BF16)


def forward_kernel(m_ref, features_ref, deg_ref, send_ref):
    n_col, rows = send_ref.shape[0], send_ref.shape[1] - 16
    size = m_ref.shape[0]
    for start in range(0, n_col, 4):
        sums = jnp.dot(
            m_ref[start * rows : (start + 4) * rows, :], features_ref[...], preferred_element_type=F32
        ).astype(BF16)
        for k in range(4):
            send_ref[start + k, :rows, :] = sums[k * rows : (k + 1) * rows, :]
    for j in range(n_col):
        base = (j // 2) * 128
        send_ref[j, rows:, :128] = deg_ref[:, base : base + 128]
        send_ref[j, rows:, 128:] = deg_ref[:, size + base : size + base + 128]


def dense_kernel(half_ref, recv_ref, weight_ref, bias_ref, cot_ref, out_ref, send_ref):
    n_col, rows = recv_ref.shape[0], recv_ref.shape[1] - 16
    sums = recv_ref[0, :rows, :].astype(F32)
    deg_parts = recv_ref[0, rows:, :].astype(F32)
    for j in range(1, n_col):
        sums += recv_ref[j, :rows, :].astype(F32)
        deg_parts += recv_ref[j, rows:, :].astype(F32)
    deg_lanes = 128.0 * deg_parts[:1, :128] + deg_parts[:1, 128:]
    lane = lax.broadcasted_iota(jnp.int32, (rows, 128), 1)
    own = lax.broadcasted_iota(jnp.int32, (rows, 128), 0) + rows * half_ref[0]
    degree = jnp.sum(jnp.where(lane == own, deg_lanes, 0.0), axis=1, keepdims=True)
    scale = lax.rsqrt(jnp.maximum(degree, 1.0))
    agg = (sums * scale).astype(BF16)
    pre = jnp.dot(agg, weight_ref[...], preferred_element_type=F32) + bias_ref[...]
    sigma = jax.nn.sigmoid(pre)
    out_ref[...] = (pre * sigma).astype(BF16)
    grad = (cot_ref[...].astype(F32) * (sigma * (1.0 + pre * (1.0 - sigma)))).astype(BF16)
    dsum = (dot_nt(grad, weight_ref[...]) * scale).astype(BF16)
    weight_term = lax.dot_general(agg, grad, TN, preferred_element_type=F32).astype(BF16)
    bias_rows = split_rows(jnp.sum(grad.astype(F32), axis=0, keepdims=True))
    for j in range(n_col):
        send_ref[j, :rows, :] = dsum
        send_ref[j, rows : rows + 16, :] = weight_term[16 * j : 16 * (j + 1), :]
        send_ref[j, rows + 16 :, :] = bias_rows


def split_rows(row):
    high = row.astype(BF16)
    low = (row - high.astype(F32)).astype(BF16)
    index = lax.broadcasted_iota(jnp.int32, (16, row.shape[1]), 0)
    both = jnp.where(index == 0, high.astype(F32), jnp.where(index == 1, low.astype(F32), 0.0))
    return both.astype(BF16)


def backward_kernel(mt_ref, recv_ref, send_ref, grads_ref):
    n_col, rows = recv_ref.shape[0], recv_ref.shape[1] - 32
    n_row, own = send_ref.shape[0], send_ref.shape[1] - 32
    extra = recv_ref[0, rows:, :].astype(F32)
    for j in range(1, n_col):
        extra += recv_ref[j, rows:, :].astype(F32)
    weight_rows = extra[:16, :].astype(BF16)
    bias_rows = split_rows(jnp.sum(extra[16:, :], axis=0, keepdims=True))
    for j in range(n_col):
        grads_ref[j * rows : (j + 1) * rows, :] = recv_ref[j, :rows, :]
    group = 8
    for start in range(0, n_row, group):
        sums = jnp.dot(
            mt_ref[start * own : (start + group) * own, :], grads_ref[...], preferred_element_type=F32
        ).astype(BF16)
        for k in range(group):
            send_ref[start + k, :own, :] = sums[k * own : (k + 1) * own, :]
    for i in range(n_row):
        send_ref[i, own : own + 16, :] = weight_rows
        send_ref[i, own + 16 :, :] = bias_rows


def final_kernel(recv_ref, feature_ref, chunk_ref, bias_ref):
    n_row, own = recv_ref.shape[0], recv_ref.shape[1] - 32
    total = recv_ref[0].astype(F32)
    for i in range(1, n_row):
        total += recv_ref[i].astype(F32)
    feature_ref[...] = total[:own, :].astype(BF16)
    chunk_ref[...] = total[own : own + 16, :]
    bias_ref[...] = jnp.sum(total[own + 16 :, :], axis=0, keepdims=True)


def exchange(blocks, axis):
    return lax.all_to_all(blocks, axis, split_axis=0, concat_axis=0, tiled=True)


def spread(block, count, axis):
    return exchange(jnp.broadcast_to(block[None], (count,) + block.shape), axis)


def make_body(n_row, n_col):
    def body(
        features,
        node_order,
        tile_weights,
        tile_rows,
        tile_cols,
        tile_count,
        weight,
        bias_vector,
        cotangent,
    ):
        own, width = features.shape[1], features.shape[2]
        size = n_row * own
        rows = cotangent.shape[0]
        gathered = spread(features[0], n_row, "row").reshape(size, width)
        matrix, matrix_t, degree = pl.pallas_call(
            edges_kernel,
            out_shape=(
                jax.ShapeDtypeStruct((size, size), BF16),
                jax.ShapeDtypeStruct((size, size), BF16),
                jax.ShapeDtypeStruct((16, 2 * size), BF16),
            ),
            in_specs=[SMEM, SMEM, SMEM, VMEM, VMEM],
            out_specs=(VMEM, VMEM, VMEM),
            scratch_shapes=[pltpu.VMEM((size, size), BF16), pltpu.VMEM((size, size), BF16)],
            compiler_params=PARAMS,
            cost_estimate=pl.CostEstimate(flops=8 * size**3, bytes_accessed=5 * 2**20, transcendentals=0),
            name="edges",
        )(tile_count, tile_rows, tile_cols, node_order, tile_weights)
        send_sums = pl.pallas_call(
            forward_kernel,
            out_shape=jax.ShapeDtypeStruct((n_col, rows + 16, width), BF16),
            in_specs=[VMEM] * 3,
            out_specs=VMEM,
            compiler_params=PARAMS,
            name="forward",
        )(matrix, gathered, degree)
        recv_sums = exchange(send_sums, "col")
        half = (lax.axis_index("col") % 2).astype(jnp.int32).reshape(1)
        output, send_grads = pl.pallas_call(
            dense_kernel,
            out_shape=(
                jax.ShapeDtypeStruct((rows, width), BF16),
                jax.ShapeDtypeStruct((n_col, rows + 32, width), BF16),
            ),
            in_specs=[SMEM] + [VMEM] * 4,
            out_specs=(VMEM, VMEM),
            compiler_params=PARAMS,
            name="dense",
        )(half, recv_sums, weight, bias_vector.reshape(1, width), cotangent)
        recv_grads = exchange(send_grads, "col")
        send_back = pl.pallas_call(
            backward_kernel,
            out_shape=jax.ShapeDtypeStruct((n_row, own + 32, width), BF16),
            in_specs=[VMEM] * 2,
            out_specs=VMEM,
            scratch_shapes=[pltpu.VMEM((size, width), BF16)],
            compiler_params=PARAMS,
            name="backward",
        )(matrix_t, recv_grads)
        recv_back = exchange(send_back, "row")
        feature_grad, chunk, bias_grad = pl.pallas_call(
            final_kernel,
            out_shape=(
                jax.ShapeDtypeStruct((own, width), BF16),
                jax.ShapeDtypeStruct((16, width), F32),
                jax.ShapeDtypeStruct((1, width), F32),
            ),
            in_specs=[VMEM],
            out_specs=(VMEM,) * 3,
            compiler_params=PARAMS,
            name="final",
        )(recv_back)
        weight_grad = spread(chunk, n_col, "col").reshape(width, width)
        return (output, feature_grad[None], weight_grad, bias_grad.reshape(width))

    return body


def solution(mesh):
    return jax.shard_map(
        make_body(mesh.shape["row"], mesh.shape["col"]),
        mesh=mesh,
        in_specs=(
            P("col", "row", None),
            P("col", None),
            P(("row", "col"), None, None),
            P(("row", "col")),
            P(("row", "col")),
            P(("row", "col")),
            P(),
            P(),
            P(("row", "col"), None),
        ),
        out_specs=(P(("row", "col"), None), P("col", "row", None), P(), P()),
        check_vma=False,
    )
```

```python
import jax
import jax.numpy as jnp
from jax import lax
from jax.experimental import pallas as pl
from jax.experimental.pallas import tpu as pltpu
from jax.sharding import Mesh, PartitionSpec as P

BF16 = jnp.bfloat16
F32 = jnp.float32
LANES = 128
HALVES = 2
NT = (((1,), (1,)), ((), ()))
TN = (((0,), (0,)), ((), ()))
VMEM = pl.BlockSpec(memory_space=pltpu.VMEM)
SMEM = pl.BlockSpec(memory_space=pltpu.SMEM)
PARAMS = pltpu.CompilerParams(vmem_limit_bytes=32 * 1024 * 1024)


def dot_nt(left, right):
    return lax.dot_general(left, right, NT, preferred_element_type=F32)


def rows_block(rows, height=8):
    index = lax.broadcasted_iota(jnp.int32, (height, LANES), 0)
    block = jnp.zeros((height, LANES), F32)
    for k, row in enumerate(rows):
        block = jnp.where(index == k, row, block)
    return block


def bias_block(row):
    high = row.astype(BF16).astype(F32)
    low = row - high
    return rows_block([high[:, :LANES], high[:, LANES:], low[:, :LANES], low[:, LANES:]]).astype(BF16)


def spread_kernel(block_ref, out_ref):
    for i in range(out_ref.shape[0]):
        out_ref[i] = block_ref[0]


def edges_kernel(count_ref, rows_ref, cols_ref, order_ref, tiles_ref, m_ref, mt_ref, deg_ref, a_ref, p_ref):
    a_ref[...] = jnp.zeros_like(a_ref)
    tile = tiles_ref.shape[1]

    def add_slot(slot, carry):
        row = pl.multiple_of(rows_ref[slot] * tile, tile)
        col = pl.multiple_of(cols_ref[slot] * tile, tile)
        a_ref[pl.ds(row, tile), pl.ds(col, tile)] += tiles_ref[slot]
        return carry

    lax.fori_loop(0, count_ref[0], add_slot, 0)
    size = a_ref.shape[0]
    order = jnp.broadcast_to(order_ref[...], (size, size))
    places = lax.broadcasted_iota(jnp.int32, (size, size), 0)
    p_ref[...] = jnp.where(places == order, 1.0, 0.0).astype(BF16)
    step = 256
    for start in range(0, size, step):
        part = slice(start, start + step)
        m_ref[:, part] = dot_nt(a_ref[...], p_ref[part, :]).astype(BF16)
        mt_ref[:, part] = dot_nt(p_ref[...], a_ref[part, :]).astype(BF16)
    degree = dot_nt(jnp.ones((16, size), BF16), a_ref[...])[:8, :]
    high = jnp.floor(degree * (1.0 / 128.0))
    index = lax.broadcasted_iota(jnp.int32, degree.shape, 0)
    deg_ref[...] = jnp.where(index == 0, high, degree - 128.0 * high).astype(BF16)


def forward_kernel(m_ref, features_ref, deg_ref, send_ref):
    n_col = send_ref.shape[0]
    rows = m_ref.shape[0] // n_col
    group = 4
    for start in range(0, n_col, group):
        sums = jnp.dot(
            m_ref[start * rows : (start + group) * rows, :], features_ref[...], preferred_element_type=F32
        ).astype(BF16)
        for k in range(group):
            send_ref[start + k, :rows, :] = sums[k * rows : (k + 1) * rows, :LANES]
            send_ref[start + k, rows : 2 * rows, :] = sums[k * rows : (k + 1) * rows, LANES:]
    for j in range(n_col):
        base = j * rows // LANES * LANES
        send_ref[j, 2 * rows :, :] = deg_ref[:, base : base + LANES]


def dense_kernel(half_ref, recv_ref, weight_ref, bias_ref, cot_ref, out_ref, send_ref):
    n_col, rows = recv_ref.shape[0], cot_ref.shape[0]
    total = recv_ref[0].astype(F32)
    for j in range(1, n_col):
        total += recv_ref[j].astype(F32)
    sums = jnp.concatenate([total[:rows, :], total[rows : 2 * rows, :]], axis=1)
    deg_lanes = 128.0 * total[2 * rows : 2 * rows + 1, :] + total[2 * rows + 1 : 2 * rows + 2, :]
    lane = lax.broadcasted_iota(jnp.int32, (rows, LANES), 1)
    own = lax.broadcasted_iota(jnp.int32, (rows, LANES), 0) + rows * half_ref[0]
    degree = jnp.sum(jnp.where(lane == own, deg_lanes, 0.0), axis=1, keepdims=True)
    scale = lax.rsqrt(jnp.maximum(degree, 1.0))
    agg = (sums * scale).astype(BF16)
    pre = jnp.dot(agg, weight_ref[...], preferred_element_type=F32) + bias_ref[...]
    sigma = jax.nn.sigmoid(pre)
    out_ref[...] = (pre * sigma).astype(BF16)
    grad = (cot_ref[...].astype(F32) * (sigma * (1.0 + pre * (1.0 - sigma)))).astype(BF16)
    dsum = (dot_nt(grad, weight_ref[...]) * scale).astype(BF16)
    weight_term = lax.dot_general(agg, grad, TN, preferred_element_type=F32)
    bias_rows = bias_block(jnp.sum(grad.astype(F32), axis=0, keepdims=True))
    part = weight_term.shape[0] // (HALVES * n_col)
    for j in range(n_col):
        chunk = jnp.concatenate(
            [weight_term[(h * n_col + j) * part : (h * n_col + j + 1) * part, :] for h in range(HALVES)], axis=0
        ).astype(BF16)
        send_ref[j, :rows, :] = dsum[:, :LANES]
        send_ref[j, rows : 2 * rows, :] = dsum[:, LANES:]
        send_ref[j, 2 * rows : 2 * rows + 16, :] = chunk[:, :LANES]
        send_ref[j, 2 * rows + 16 : 2 * rows + 32, :] = chunk[:, LANES:]
        send_ref[j, 2 * rows + 32 :, :] = bias_rows


def backward_kernel(mt_ref, recv_ref, send_ref, grads_ref):
    n_col, n_row = recv_ref.shape[0], send_ref.shape[0]
    size = mt_ref.shape[0]
    rows, own = size // n_col, size // n_row
    extra = recv_ref[0, 2 * rows :, :].astype(F32)
    for j in range(1, n_col):
        extra += recv_ref[j, 2 * rows :, :].astype(F32)
    bias = extra[32:34, :] + extra[34:36, :]
    bias_rows = bias_block(jnp.concatenate([bias[:1, :], bias[1:, :]], axis=1))
    for j in range(n_col):
        grads_ref[j * rows : (j + 1) * rows, :LANES] = recv_ref[j, :rows, :]
        grads_ref[j * rows : (j + 1) * rows, LANES:] = recv_ref[j, rows : 2 * rows, :]
    group = 8
    for start in range(0, n_row, group):
        sums = jnp.dot(
            mt_ref[start * own : (start + group) * own, :], grads_ref[...], preferred_element_type=F32
        ).astype(BF16)
        for k in range(group):
            send_ref[start + k, :own, :] = sums[k * own : (k + 1) * own, :LANES]
            send_ref[start + k, own : 2 * own, :] = sums[k * own : (k + 1) * own, LANES:]
    for h in range(HALVES):
        chunk = jnp.concatenate([extra[8 * h : 8 * h + 8, :], extra[16 + 8 * h : 24 + 8 * h, :]], axis=0).astype(BF16)
        for z in range(n_row // HALVES):
            send_ref[h * (n_row // HALVES) + z, 2 * own : 2 * own + 16, :] = chunk
    for i in range(n_row):
        send_ref[i, 2 * own + 16 :, :] = bias_rows


def final_kernel(recv_ref, feature_ref, bias_ref, spread_ref):
    n_row, own = recv_ref.shape[0], feature_ref.shape[0]
    total = recv_ref[0].astype(F32)
    for i in range(1, n_row):
        total += recv_ref[i].astype(F32)
    feature_ref[:, :LANES] = total[:own, :].astype(BF16)
    feature_ref[:, LANES:] = total[own : 2 * own, :].astype(BF16)
    base = 2 * own
    chunk = jnp.concatenate([total[base : base + 8, :], total[base + 8 : base + 16, :]], axis=1)
    for i in range(spread_ref.shape[0]):
        spread_ref[i] = chunk
    bias = total[base + 16 : base + 18, :] + total[base + 18 : base + 20, :]
    bias_ref[:, :LANES] = bias[:1, :]
    bias_ref[:, LANES:] = bias[1:, :]


def exchange(blocks, axes):
    return lax.all_to_all(blocks, axes, split_axis=0, concat_axis=0, tiled=True)


def call(kernel, out_shape, in_specs, scratch=(), **options):
    several = isinstance(out_shape, tuple)
    return pl.pallas_call(
        kernel,
        out_shape=out_shape,
        in_specs=in_specs,
        out_specs=(VMEM,) * len(out_shape) if several else VMEM,
        scratch_shapes=list(scratch),
        compiler_params=PARAMS,
        name=kernel.__name__,
        **options,
    )


def make_body(n_row, n_col):
    row_axes = ("half", "rest")

    def body(
        features,
        node_order,
        tile_weights,
        tile_rows,
        tile_cols,
        tile_count,
        weight,
        bias_vector,
        cotangent,
    ):
        own, width = features.shape[1], features.shape[2]
        size = n_row * own
        rows = cotangent.shape[0]
        shape = jax.ShapeDtypeStruct
        sends = call(spread_kernel, shape((n_row, own, width), BF16), [VMEM])(features)
        gathered = exchange(sends, row_axes).reshape(size, width)
        matrix, matrix_t, degree = call(
            edges_kernel,
            (shape((size, size), BF16), shape((size, size), BF16), shape((8, size), BF16)),
            [SMEM, SMEM, SMEM, VMEM, VMEM],
            [pltpu.VMEM((size, size), BF16), pltpu.VMEM((size, size), BF16)],
            cost_estimate=pl.CostEstimate(flops=8 * size**3, bytes_accessed=5 * 2**20, transcendentals=0),
        )(tile_count, tile_rows, tile_cols, node_order, tile_weights)
        send_sums = call(forward_kernel, shape((n_col, 2 * rows + 8, LANES), BF16), [VMEM] * 3)(
            matrix, gathered, degree
        )
        recv_sums = exchange(send_sums, "col")
        half = (lax.axis_index("col") * rows % LANES // rows).astype(jnp.int32).reshape(1)
        output, send_grads = call(
            dense_kernel,
            (shape((rows, width), BF16), shape((n_col, 2 * rows + 40, LANES), BF16)),
            [SMEM] + [VMEM] * 4,
        )(half, recv_sums, weight, bias_vector.reshape(1, width), cotangent)
        recv_grads = exchange(send_grads, "col")
        send_back = call(
            backward_kernel,
            shape((n_row, 2 * own + 24, LANES), BF16),
            [VMEM] * 2,
            [pltpu.VMEM((size, width), BF16)],
        )(matrix_t, recv_grads)
        recv_back = exchange(send_back, row_axes)
        feature_grad, bias_grad, send_weight = call(
            final_kernel,
            (
                shape((own, width), BF16),
                shape((1, width), F32),
                shape((HALVES * n_col, 8, width), F32),
            ),
            [VMEM],
        )(recv_back)
        weight_grad = exchange(send_weight, ("half", "col")).reshape(width, width)
        return (output, feature_grad[None], weight_grad, bias_grad.reshape(width))

    return body


def solution(mesh):
    n_row, n_col = mesh.shape["row"], mesh.shape["col"]
    row = ("half", "rest")
    split = Mesh(mesh.devices.reshape(HALVES, n_row // HALVES, n_col), row + ("col",))
    return jax.shard_map(
        make_body(n_row, n_col),
        mesh=split,
        in_specs=(
            P("col", row, None),
            P("col", None),
            P(row + ("col",), None, None),
            P(row + ("col",)),
            P(row + ("col",)),
            P(row + ("col",)),
            P(),
            P(),
            P(row + ("col",), None),
        ),
        out_specs=(P(row + ("col",), None), P("col", row, None), P(), P()),
        check_vma=False,
    )
```

```python
import jax
import jax.numpy as jnp
from jax import lax
from jax.experimental import pallas as pl
from jax.experimental.pallas import tpu as pltpu
from jax.sharding import Mesh, PartitionSpec as P

BF16 = jnp.bfloat16
F32 = jnp.float32
LANES = 128
HALVES, FAR, NEAR = 2, 8, 2
NT = (((1,), (1,)), ((), ()))
TN = (((0,), (0,)), ((), ()))
VMEM = pl.BlockSpec(memory_space=pltpu.VMEM)
SMEM = pl.BlockSpec(memory_space=pltpu.SMEM)
PARAMS = pltpu.CompilerParams(vmem_limit_bytes=32 * 1024 * 1024)


def dot_nt(left, right):
    return lax.dot_general(left, right, NT, preferred_element_type=F32)


def rows_block(rows, height=8):
    index = lax.broadcasted_iota(jnp.int32, (height, LANES), 0)
    block = jnp.zeros((height, LANES), F32)
    for k, row in enumerate(rows):
        block = jnp.where(index == k, row, block)
    return block


def bias_block(row):
    high = row.astype(BF16).astype(F32)
    low = row - high
    return rows_block([high[:, :LANES], high[:, LANES:], low[:, :LANES], low[:, LANES:]]).astype(BF16)


def spread_kernel(block_ref, out_ref):
    for i in range(out_ref.shape[0]):
        out_ref[i] = block_ref[...].reshape(out_ref.shape[1:])


def exchanged_place(place, own):
    low, block = place & (own - 1), place >> (own.bit_length() - 1)
    near, block = block & (NEAR - 1), block >> (NEAR.bit_length() - 1)
    far, half = block & (FAR - 1), block >> (FAR.bit_length() - 1)
    return ((half * NEAR + near) * FAR + far) * own + low


def edges_kernel(count_ref, rows_ref, cols_ref, order_ref, tiles_ref, m_ref, mt_ref, deg_ref, a_ref, p_ref):
    a_ref[...] = jnp.zeros_like(a_ref)
    tile = tiles_ref.shape[1]

    def add_slot(slot, carry):
        row = pl.multiple_of(rows_ref[slot] * tile, tile)
        col = pl.multiple_of(cols_ref[slot] * tile, tile)
        a_ref[pl.ds(row, tile), pl.ds(col, tile)] += tiles_ref[slot]
        return carry

    lax.fori_loop(0, count_ref[0], add_slot, 0)
    size = a_ref.shape[0]
    own = size // (HALVES * FAR * NEAR)
    order = jnp.broadcast_to(exchanged_place(order_ref[...], own), (size, size))
    places = lax.broadcasted_iota(jnp.int32, (size, size), 0)
    p_ref[...] = jnp.where(places == order, 1.0, 0.0).astype(BF16)
    step = 256
    for start in range(0, size, step):
        part = slice(start, start + step)
        m_ref[:, part] = dot_nt(a_ref[...], p_ref[part, :]).astype(BF16)
        mt_ref[:, part] = dot_nt(p_ref[...], a_ref[part, :]).astype(BF16)
    degree = dot_nt(jnp.ones((16, size), BF16), a_ref[...])[:8, :]
    high = jnp.floor(degree * (1.0 / 128.0))
    index = lax.broadcasted_iota(jnp.int32, degree.shape, 0)
    deg_ref[...] = jnp.where(index == 0, high, degree - 128.0 * high).astype(BF16)


def forward_kernel(m_ref, features_ref, deg_ref, send_ref):
    n_col = send_ref.shape[0]
    rows = m_ref.shape[0] // n_col
    group = 4
    for start in range(0, n_col, group):
        sums = jnp.dot(
            m_ref[start * rows : (start + group) * rows, :], features_ref[...], preferred_element_type=F32
        ).astype(BF16)
        for k in range(group):
            send_ref[start + k, :rows, :] = sums[k * rows : (k + 1) * rows, :LANES]
            send_ref[start + k, rows : 2 * rows, :] = sums[k * rows : (k + 1) * rows, LANES:]
    for j in range(n_col):
        base = j * rows // LANES * LANES
        send_ref[j, 2 * rows :, :] = deg_ref[:, base : base + LANES]


def dense_kernel(half_ref, recv_ref, weight_ref, bias_ref, cot_ref, out_ref, send_ref):
    n_col, rows = recv_ref.shape[0], cot_ref.shape[0]
    total = recv_ref[0].astype(F32)
    for j in range(1, n_col):
        total += recv_ref[j].astype(F32)
    sums = jnp.concatenate([total[:rows, :], total[rows : 2 * rows, :]], axis=1)
    deg_lanes = 128.0 * total[2 * rows : 2 * rows + 1, :] + total[2 * rows + 1 : 2 * rows + 2, :]
    lane = lax.broadcasted_iota(jnp.int32, (rows, LANES), 1)
    own = lax.broadcasted_iota(jnp.int32, (rows, LANES), 0) + rows * half_ref[0]
    degree = jnp.sum(jnp.where(lane == own, deg_lanes, 0.0), axis=1, keepdims=True)
    scale = lax.rsqrt(jnp.maximum(degree, 1.0))
    agg = (sums * scale).astype(BF16)
    pre = jnp.dot(agg, weight_ref[...], preferred_element_type=F32) + bias_ref[...]
    sigma = jax.nn.sigmoid(pre)
    out_ref[...] = (pre * sigma).astype(BF16)
    grad = (cot_ref[...].astype(F32) * (sigma * (1.0 + pre * (1.0 - sigma)))).astype(BF16)
    dsum = (dot_nt(grad, weight_ref[...]) * scale).astype(BF16)
    weight_term = lax.dot_general(agg, grad, TN, preferred_element_type=F32)
    bias_rows = bias_block(jnp.sum(grad.astype(F32), axis=0, keepdims=True))
    weight_term = weight_term.astype(BF16)
    for j in range(n_col):
        chunk = weight_term[16 * j : 16 * (j + 1), :]
        send_ref[j, :rows, :] = dsum[:, :LANES]
        send_ref[j, rows : 2 * rows, :] = dsum[:, LANES:]
        send_ref[j, 2 * rows : 2 * rows + 16, :] = chunk[:, :LANES]
        send_ref[j, 2 * rows + 16 : 2 * rows + 32, :] = chunk[:, LANES:]
        send_ref[j, 2 * rows + 32 :, :] = bias_rows


def backward_kernel(mt_ref, recv_ref, send_ref, grads_ref):
    n_col, n_near = recv_ref.shape[0], send_ref.shape[0]
    size = mt_ref.shape[0]
    rows, own = size // n_col, size // (n_near * FAR)
    extra = recv_ref[0, 2 * rows :, :].astype(F32)
    for j in range(1, n_col):
        extra += recv_ref[j, 2 * rows :, :].astype(F32)
    chunk = extra[:32, :].astype(BF16)
    bias_rows = merged_bias(extra[32:, :])
    for j in range(n_col):
        grads_ref[j * rows : (j + 1) * rows, :LANES] = recv_ref[j, :rows, :]
        grads_ref[j * rows : (j + 1) * rows, LANES:] = recv_ref[j, rows : 2 * rows, :]
    for i in range(n_near):
        sums = jnp.dot(
            mt_ref[i * FAR * own : (i + 1) * FAR * own, :], grads_ref[...], preferred_element_type=F32
        ).astype(BF16)
        for k in range(FAR):
            base = 2 * own * k
            send_ref[i, base : base + own, :] = sums[k * own : (k + 1) * own, :LANES]
            send_ref[i, base + own : base + 2 * own, :] = sums[k * own : (k + 1) * own, LANES:]
        send_ref[i, 2 * own * FAR : 2 * own * FAR + 32, :] = chunk
        send_ref[i, 2 * own * FAR + 32 :, :] = bias_rows


def merged_bias(rows):
    bias = rows[:2, :] + rows[2:4, :]
    return bias_block(jnp.concatenate([bias[:1, :], bias[1:, :]], axis=1))


def middle_kernel(recv_ref, send_ref):
    part = (recv_ref.shape[1] - 40) // FAR
    total = recv_ref[0].astype(F32)
    for i in range(1, recv_ref.shape[0]):
        total += recv_ref[i].astype(F32)
    base = part * FAR
    chunk = total[base : base + 32, :].astype(BF16)
    bias_rows = merged_bias(total[base + 32 :, :])
    for k in range(FAR):
        send_ref[k, :part, :] = total[k * part : (k + 1) * part, :].astype(BF16)
        send_ref[k, part : part + 32, :] = chunk
        send_ref[k, part + 32 :, :] = bias_rows


def final_kernel(recv_ref, feature_ref, bias_ref, spread_ref):
    own = feature_ref.shape[0]
    total = recv_ref[0].astype(F32)
    for i in range(1, recv_ref.shape[0]):
        total += recv_ref[i].astype(F32)
    feature_ref[:, :LANES] = total[:own, :].astype(BF16)
    feature_ref[:, LANES:] = total[own : 2 * own, :].astype(BF16)
    base = 2 * own
    for i in range(spread_ref.shape[0]):
        spread_ref[i, :, :LANES] = total[base : base + 16, :]
        spread_ref[i, :, LANES:] = total[base + 16 : base + 32, :]
    bias = total[base + 32 : base + 34, :] + total[base + 34 : base + 36, :]
    bias_ref[:, :LANES] = bias[:1, :]
    bias_ref[:, LANES:] = bias[1:, :]


def exchange(blocks, axes):
    return lax.all_to_all(blocks, axes, split_axis=0, concat_axis=0, tiled=True)


def call(kernel, out_shape, in_specs, scratch=(), **options):
    several = isinstance(out_shape, tuple)
    return pl.pallas_call(
        kernel,
        out_shape=out_shape,
        in_specs=in_specs,
        out_specs=(VMEM,) * len(out_shape) if several else VMEM,
        scratch_shapes=list(scratch),
        compiler_params=PARAMS,
        name=kernel.__name__,
        **options,
    )


def make_body(n_row, n_col):
    near_axes = ("half", "near")
    n_near = HALVES * NEAR

    def body(
        features,
        node_order,
        tile_weights,
        tile_rows,
        tile_cols,
        tile_count,
        weight,
        bias_vector,
        cotangent,
    ):
        own, width = features.shape[1], features.shape[2]
        size = n_row * own
        rows = cotangent.shape[0]
        shape = jax.ShapeDtypeStruct
        sends = call(spread_kernel, shape((FAR, own, width), BF16), [VMEM])(features)
        some = exchange(sends, "far")
        sends = call(spread_kernel, shape((n_near, FAR * own, width), BF16), [VMEM])(some)
        gathered = exchange(sends, near_axes).reshape(size, width)
        matrix, matrix_t, degree = call(
            edges_kernel,
            (shape((size, size), BF16), shape((size, size), BF16), shape((8, size), BF16)),
            [SMEM, SMEM, SMEM, VMEM, VMEM],
            [pltpu.VMEM((size, size), BF16), pltpu.VMEM((size, size), BF16)],
            cost_estimate=pl.CostEstimate(flops=8 * size**3, bytes_accessed=5 * 2**20, transcendentals=0),
        )(tile_count, tile_rows, tile_cols, node_order, tile_weights)
        send_sums = call(forward_kernel, shape((n_col, 2 * rows + 8, LANES), BF16), [VMEM] * 3)(
            matrix, gathered, degree
        )
        recv_sums = exchange(send_sums, "col")
        half = (lax.axis_index("col") * rows % LANES // rows).astype(jnp.int32).reshape(1)
        output, send_grads = call(
            dense_kernel,
            (shape((rows, width), BF16), shape((n_col, 2 * rows + 40, LANES), BF16)),
            [SMEM] + [VMEM] * 4,
        )(half, recv_sums, weight, bias_vector.reshape(1, width), cotangent)
        recv_grads = exchange(send_grads, "col")
        send_back = call(
            backward_kernel,
            shape((n_near, 2 * own * FAR + 40, LANES), BF16),
            [VMEM] * 2,
            [pltpu.VMEM((size, width), BF16)],
        )(matrix_t, recv_grads)
        recv_near = exchange(send_back, near_axes)
        send_far = call(middle_kernel, shape((FAR, 2 * own + 40, LANES), BF16), [VMEM])(recv_near)
        recv_back = exchange(send_far, "far")
        feature_grad, bias_grad, send_weight = call(
            final_kernel,
            (
                shape((own, width), BF16),
                shape((1, width), F32),
                shape((n_col, 16, width), F32),
            ),
            [VMEM],
        )(recv_back)
        weight_grad = exchange(send_weight, "col").reshape(width, width)
        return (output, feature_grad[None], weight_grad, bias_grad.reshape(width))

    return body


def solution(mesh):
    n_row, n_col = mesh.shape["row"], mesh.shape["col"]
    row = ("half", "far", "near")
    split = Mesh(mesh.devices.reshape(HALVES, FAR, NEAR, n_col), row + ("col",))
    return jax.shard_map(
        make_body(n_row, n_col),
        mesh=split,
        in_specs=(
            P("col", row, None),
            P("col", None),
            P(row + ("col",), None, None),
            P(row + ("col",)),
            P(row + ("col",)),
            P(row + ("col",)),
            P(),
            P(),
            P(row + ("col",), None),
        ),
        out_specs=(P(row + ("col",), None), P("col", row, None), P(), P()),
        check_vma=False,
    )
```

```python
import jax
import jax.numpy as jnp
from jax import lax
from jax.experimental import pallas as pl
from jax.experimental.pallas import tpu as pltpu
from jax.sharding import Mesh, PartitionSpec as P

BF16 = jnp.bfloat16
F32 = jnp.float32
LANES = 128
HALVES, FAR, NEAR = 2, 8, 2
NT = (((1,), (1,)), ((), ()))
TN = (((0,), (0,)), ((), ()))
VMEM = pl.BlockSpec(memory_space=pltpu.VMEM)
SMEM = pl.BlockSpec(memory_space=pltpu.SMEM)


def dot_nt(left, right):
    return lax.dot_general(left, right, NT, preferred_element_type=F32)


def rows_block(rows, height=8):
    index = lax.broadcasted_iota(jnp.int32, (height, LANES), 0)
    block = jnp.zeros((height, LANES), F32)
    for k, row in enumerate(rows):
        block = jnp.where(index == k, row, block)
    return block


def bias_block(row):
    high = row.astype(BF16).astype(F32)
    low = row - high
    return rows_block([high[:, :LANES], high[:, LANES:], low[:, :LANES], low[:, LANES:]]).astype(BF16)


def spread_kernel(block_ref, out_ref):
    for i in range(out_ref.shape[0]):
        out_ref[i] = block_ref[...].reshape(out_ref.shape[1:])


def exchanged_place(place, own):
    low, block = place & (own - 1), place >> (own.bit_length() - 1)
    near, block = block & (NEAR - 1), block >> (NEAR.bit_length() - 1)
    far, half = block & (FAR - 1), block >> (FAR.bit_length() - 1)
    return ((half * NEAR + near) * FAR + far) * own + low


def edges_kernel(count_ref, rows_ref, cols_ref, order_ref, tiles_ref, m_ref, deg_ref, a_ref, p_ref):
    a_ref[...] = jnp.zeros_like(a_ref)
    tile = tiles_ref.shape[1]

    def add_slot(slot, carry):
        row = pl.multiple_of(rows_ref[slot] * tile, tile)
        col = pl.multiple_of(cols_ref[slot] * tile, tile)
        a_ref[pl.ds(row, tile), pl.ds(col, tile)] += tiles_ref[slot]
        return carry

    lax.fori_loop(0, count_ref[0], add_slot, 0)
    size = a_ref.shape[0]
    own = size // (HALVES * FAR * NEAR)
    order = jnp.broadcast_to(exchanged_place(order_ref[...], own), (size, size))
    places = lax.broadcasted_iota(jnp.int32, (size, size), 0)
    p_ref[...] = jnp.where(places == order, 1.0, 0.0).astype(BF16)
    step = 256
    for start in range(0, size, step):
        part = slice(start, start + step)
        m_ref[:, part] = dot_nt(a_ref[...], p_ref[part, :]).astype(BF16)
    degree = dot_nt(jnp.ones((16, size), BF16), a_ref[...])[:8, :]
    high = jnp.floor(degree * (1.0 / 128.0))
    index = lax.broadcasted_iota(jnp.int32, degree.shape, 0)
    pairs = jnp.where(index == 0, high, degree - 128.0 * high)
    rows = size * LANES // deg_ref.shape[1]
    for j in range(size // rows):
        block = pairs[:, j * rows // LANES * LANES :][:, :LANES]
        first = j * rows % LANES
        if first:
            block = jnp.concatenate([block[:, first:], block[:, :first]], axis=1)
        deg_ref[:, j * LANES : (j + 1) * LANES] = block.astype(BF16)


def forward_kernel(m_ref, features_ref, deg_ref, send_ref):
    n_col = send_ref.shape[0]
    rows = m_ref.shape[0] // n_col
    group = 4
    for start in range(0, n_col, group):
        sums = jnp.dot(
            m_ref[start * rows : (start + group) * rows, :], features_ref[...], preferred_element_type=F32
        ).astype(BF16)
        for k in range(group):
            send_ref[start + k, :rows, :] = sums[k * rows : (k + 1) * rows, :LANES]
            send_ref[start + k, rows : 2 * rows, :] = sums[k * rows : (k + 1) * rows, LANES:]
    for j in range(n_col):
        send_ref[j, 2 * rows :, :] = deg_ref[:, j * LANES : (j + 1) * LANES]


def dense_kernel(recv_ref, weight_ref, bias_ref, cot_ref, out_ref, send_ref):
    n_col, rows = recv_ref.shape[0], cot_ref.shape[0]
    total = recv_ref[0].astype(F32)
    for j in range(1, n_col):
        total += recv_ref[j].astype(F32)
    sums = jnp.concatenate([total[:rows, :], total[rows : 2 * rows, :]], axis=1)
    deg_lanes = 128.0 * total[2 * rows : 2 * rows + 1, :] + total[2 * rows + 1 : 2 * rows + 2, :]
    lane = lax.broadcasted_iota(jnp.int32, (rows, LANES), 1)
    own = lax.broadcasted_iota(jnp.int32, (rows, LANES), 0)
    degree = jnp.sum(jnp.where(lane == own, deg_lanes, 0.0), axis=1, keepdims=True)
    scale = lax.rsqrt(jnp.maximum(degree, 1.0))
    agg = (sums * scale).astype(BF16)
    pre = jnp.dot(agg, weight_ref[...], preferred_element_type=F32) + bias_ref[...]
    sigma = jax.nn.sigmoid(pre)
    out_ref[...] = (pre * sigma).astype(BF16)
    grad = (cot_ref[...].astype(F32) * (sigma * (1.0 + pre * (1.0 - sigma)))).astype(BF16)
    dsum = (dot_nt(grad, weight_ref[...]) * scale).astype(BF16)
    weight_term = lax.dot_general(agg, grad, TN, preferred_element_type=F32)
    bias_rows = bias_block(jnp.sum(grad.astype(F32), axis=0, keepdims=True))
    weight_term = weight_term.astype(BF16)
    for j in range(n_col):
        chunk = weight_term[16 * j : 16 * (j + 1), :]
        send_ref[j, :rows, :] = dsum[:, :LANES]
        send_ref[j, rows : 2 * rows, :] = dsum[:, LANES:]
        send_ref[j, 2 * rows : 2 * rows + 16, :] = chunk[:, :LANES]
        send_ref[j, 2 * rows + 16 : 2 * rows + 32, :] = chunk[:, LANES:]
        send_ref[j, 2 * rows + 32 :, :] = bias_rows


def backward_kernel(m_ref, recv_ref, send_ref, grads_ref):
    n_col, n_near = recv_ref.shape[0], send_ref.shape[0]
    size, width = m_ref.shape[0], grads_ref.shape[1]
    rows, own = size // n_col, size // (n_near * FAR)
    extra = recv_ref[0, 2 * rows :, :].astype(F32)
    for j in range(1, n_col):
        extra += recv_ref[j, 2 * rows :, :].astype(F32)
    chunk = extra[:32, :].astype(BF16)
    bias_rows = merged_bias(extra[32:, :])
    for j in range(n_col):
        grads_ref[j * rows : (j + 1) * rows, :LANES] = recv_ref[j, :rows, :]
        grads_ref[j * rows : (j + 1) * rows, LANES:] = recv_ref[j, rows : 2 * rows, :]
    index = lax.broadcasted_iota(jnp.int32, (width, width), 0)
    unit = jnp.where(index == lax.broadcasted_iota(jnp.int32, (width, width), 1), 1.0, 0.0).astype(BF16)
    turned = dot_nt(unit, grads_ref[...]).astype(BF16)
    for i in range(n_near):
        part = m_ref[:, i * FAR * own : (i + 1) * FAR * own]
        sums = jnp.dot(turned, part, preferred_element_type=F32).astype(BF16)
        sums = lax.dot_general(unit, sums, NT, preferred_element_type=F32).astype(BF16)
        for k in range(FAR):
            base = 2 * own * k
            send_ref[i, base : base + own, :] = sums[k * own : (k + 1) * own, :LANES]
            send_ref[i, base + own : base + 2 * own, :] = sums[k * own : (k + 1) * own, LANES:]
        send_ref[i, 2 * own * FAR : 2 * own * FAR + 32, :] = chunk
        send_ref[i, 2 * own * FAR + 32 :, :] = bias_rows


def merged_bias(rows):
    bias = rows[:2, :] + rows[2:4, :]
    return bias_block(jnp.concatenate([bias[:1, :], bias[1:, :]], axis=1))


def middle_kernel(recv_ref, send_ref):
    part = (recv_ref.shape[1] - 40) // FAR
    total = recv_ref[0].astype(F32)
    for i in range(1, recv_ref.shape[0]):
        total += recv_ref[i].astype(F32)
    base = part * FAR
    chunk = total[base : base + 32, :].astype(BF16)
    bias_rows = merged_bias(total[base + 32 :, :])
    for k in range(FAR):
        send_ref[k, :part, :] = total[k * part : (k + 1) * part, :].astype(BF16)
        send_ref[k, part : part + 32, :] = chunk
        send_ref[k, part + 32 :, :] = bias_rows


def final_kernel(recv_ref, feature_ref, bias_ref, spread_ref):
    own = feature_ref.shape[0]
    total = recv_ref[0].astype(F32)
    for i in range(1, recv_ref.shape[0]):
        total += recv_ref[i].astype(F32)
    feature_ref[:, :LANES] = total[:own, :].astype(BF16)
    feature_ref[:, LANES:] = total[own : 2 * own, :].astype(BF16)
    base = 2 * own
    for i in range(spread_ref.shape[0]):
        spread_ref[i, :, :LANES] = total[base : base + 16, :]
        spread_ref[i, :, LANES:] = total[base + 16 : base + 32, :]
    bias = total[base + 32 : base + 34, :] + total[base + 34 : base + 36, :]
    bias_ref[:, :LANES] = bias[:1, :]
    bias_ref[:, LANES:] = bias[1:, :]


def exchange(blocks, axes):
    return lax.all_to_all(blocks, axes, split_axis=0, concat_axis=0, tiled=True)


def call(kernel, out_shape, in_specs, scratch=(), vmem=8, **options):
    several = isinstance(out_shape, tuple)
    return pl.pallas_call(
        kernel,
        out_shape=out_shape,
        in_specs=in_specs,
        out_specs=(VMEM,) * len(out_shape) if several else VMEM,
        scratch_shapes=list(scratch),
        compiler_params=pltpu.CompilerParams(vmem_limit_bytes=vmem * 2**20),
        name=kernel.__name__,
        **options,
    )


def make_body(n_row, n_col):
    near_axes = ("half", "near")
    n_near = HALVES * NEAR

    def body(
        features,
        node_order,
        tile_weights,
        tile_rows,
        tile_cols,
        tile_count,
        weight,
        bias_vector,
        cotangent,
    ):
        own, width = features.shape[1], features.shape[2]
        size = n_row * own
        rows = cotangent.shape[0]
        shape = jax.ShapeDtypeStruct
        sends = call(spread_kernel, shape((FAR, own, width), BF16), [VMEM])(features)
        some = exchange(sends, "far")
        matrix, degree = call(
            edges_kernel,
            (shape((size, size), BF16), shape((8, n_col * LANES), BF16)),
            [SMEM, SMEM, SMEM, VMEM, VMEM],
            [pltpu.VMEM((size, size), BF16), pltpu.VMEM((size, size), BF16)],
            vmem=12,
            cost_estimate=pl.CostEstimate(flops=4 * size**3, bytes_accessed=3 * 2**20, transcendentals=0),
        )(tile_count, tile_rows, tile_cols, node_order, tile_weights)
        sends = call(spread_kernel, shape((n_near, FAR * own, width), BF16), [VMEM])(some)
        gathered = exchange(sends, near_axes).reshape(size, width)
        send_sums = call(forward_kernel, shape((n_col, 2 * rows + 8, LANES), BF16), [VMEM] * 3)(
            matrix, gathered, degree
        )
        recv_sums = exchange(send_sums, "col")
        output, send_grads = call(
            dense_kernel,
            (shape((rows, width), BF16), shape((n_col, 2 * rows + 40, LANES), BF16)),
            [VMEM] * 4,
        )(recv_sums, weight, bias_vector.reshape(1, width), cotangent)
        recv_grads = exchange(send_grads, "col")
        send_back = call(
            backward_kernel,
            shape((n_near, 2 * own * FAR + 40, LANES), BF16),
            [VMEM] * 2,
            [pltpu.VMEM((size, width), BF16)],
        )(matrix, recv_grads)
        recv_near = exchange(send_back, near_axes)
        send_far = call(middle_kernel, shape((FAR, 2 * own + 40, LANES), BF16), [VMEM])(recv_near)
        recv_back = exchange(send_far, "far")
        feature_grad, bias_grad, send_weight = call(
            final_kernel,
            (
                shape((own, width), BF16),
                shape((1, width), F32),
                shape((n_col, 16, width), F32),
            ),
            [VMEM],
        )(recv_back)
        weight_grad = exchange(send_weight, "col").reshape(width, width)
        return (output, feature_grad[None], weight_grad, bias_grad.reshape(width))

    return body


def solution(mesh):
    n_row, n_col = mesh.shape["row"], mesh.shape["col"]
    row = ("half", "far", "near")
    split = Mesh(mesh.devices.reshape(HALVES, FAR, NEAR, n_col), row + ("col",))
    return jax.shard_map(
        make_body(n_row, n_col),
        mesh=split,
        in_specs=(
            P("col", row, None),
            P("col", None),
            P(row + ("col",), None, None),
            P(row + ("col",)),
            P(row + ("col",)),
            P(row + ("col",)),
            P(),
            P(),
            P(row + ("col",), None),
        ),
        out_specs=(P(row + ("col",), None), P("col", row, None), P(), P()),
        check_vma=False,
    )
```

```python
import jax
import jax.numpy as jnp
from jax import lax
from jax.experimental import pallas as pl
from jax.experimental.pallas import tpu as pltpu
from jax.sharding import Mesh, PartitionSpec as P

BF16 = jnp.bfloat16
F32 = jnp.float32
LANES = 128
HALVES, FAR, NEAR = 2, 8, 2
NT = (((1,), (1,)), ((), ()))
TN = (((0,), (0,)), ((), ()))
VMEM = pl.BlockSpec(memory_space=pltpu.VMEM)
SMEM = pl.BlockSpec(memory_space=pltpu.SMEM)


def dot_nt(left, right):
    return lax.dot_general(left, right, NT, preferred_element_type=F32)


def rows_block(rows, height=8):
    index = lax.broadcasted_iota(jnp.int32, (height, LANES), 0)
    block = jnp.zeros((height, LANES), F32)
    for k, row in enumerate(rows):
        block = jnp.where(index == k, row, block)
    return block


def bias_block(row):
    high = row.astype(BF16).astype(F32)
    low = row - high
    return rows_block([high[:, :LANES], high[:, LANES:], low[:, :LANES], low[:, LANES:]]).astype(BF16)


def spread_kernel(block_ref, out_ref):
    for i in range(out_ref.shape[0]):
        out_ref[i] = block_ref[...].reshape(out_ref.shape[1:])


def exchanged_place(place, own):
    low, block = place & (own - 1), place >> (own.bit_length() - 1)
    near, block = block & (NEAR - 1), block >> (NEAR.bit_length() - 1)
    far, half = block & (FAR - 1), block >> (FAR.bit_length() - 1)
    return ((half * NEAR + near) * FAR + far) * own + low


def edges_kernel(count_ref, rows_ref, cols_ref, order_ref, tiles_ref, m_ref, deg_ref, a_ref, p_ref):
    a_ref[...] = jnp.zeros_like(a_ref)
    tile = tiles_ref.shape[1]

    def add_slot(slot, carry):
        row = pl.multiple_of(rows_ref[slot] * tile, tile)
        col = pl.multiple_of(cols_ref[slot] * tile, tile)
        a_ref[pl.ds(row, tile), pl.ds(col, tile)] += tiles_ref[slot]
        return carry

    lax.fori_loop(0, count_ref[0], add_slot, 0)
    size = a_ref.shape[0]
    own = size // (HALVES * FAR * NEAR)
    order = jnp.broadcast_to(exchanged_place(order_ref[...], own), (size, size))
    places = lax.broadcasted_iota(jnp.int32, (size, size), 0)
    p_ref[...] = jnp.where(places == order, 1.0, 0.0).astype(BF16)
    step = 256
    for start in range(0, size, step):
        part = slice(start, start + step)
        m_ref[:, part] = dot_nt(a_ref[...], p_ref[part, :]).astype(BF16)
    degree = dot_nt(jnp.ones((16, size), BF16), a_ref[...])[:8, :]
    high = jnp.floor(degree * (1.0 / 128.0))
    index = lax.broadcasted_iota(jnp.int32, degree.shape, 0)
    pairs = jnp.where(index == 0, high, degree - 128.0 * high)
    rows = size * LANES // deg_ref.shape[1]
    for j in range(size // rows):
        block = pairs[:, j * rows // LANES * LANES :][:, :LANES]
        first = j * rows % LANES
        if first:
            block = jnp.concatenate([block[:, first:], block[:, :first]], axis=1)
        deg_ref[:, j * LANES : (j + 1) * LANES] = block.astype(BF16)


def forward_kernel(m_ref, features_ref, deg_ref, send_ref):
    n_col = send_ref.shape[0]
    rows = m_ref.shape[0] // n_col
    group = 4
    for start in range(0, n_col, group):
        sums = jnp.dot(
            m_ref[start * rows : (start + group) * rows, :], features_ref[...], preferred_element_type=F32
        ).astype(BF16)
        for k in range(group):
            send_ref[start + k, :rows, :] = sums[k * rows : (k + 1) * rows, :LANES]
            send_ref[start + k, rows : 2 * rows, :] = sums[k * rows : (k + 1) * rows, LANES:]
    for j in range(n_col):
        send_ref[j, 2 * rows :, :] = deg_ref[:, j * LANES : (j + 1) * LANES]


def dense_kernel(recv_ref, weight_ref, bias_ref, cot_ref, out_ref, send_ref):
    n_col, rows = recv_ref.shape[0], cot_ref.shape[0]
    total = recv_ref[0].astype(F32)
    for j in range(1, n_col):
        total += recv_ref[j].astype(F32)
    sums = jnp.concatenate([total[:rows, :], total[rows : 2 * rows, :]], axis=1)
    deg_lanes = 128.0 * total[2 * rows : 2 * rows + 1, :] + total[2 * rows + 1 : 2 * rows + 2, :]
    lane = lax.broadcasted_iota(jnp.int32, (rows, LANES), 1)
    own = lax.broadcasted_iota(jnp.int32, (rows, LANES), 0)
    degree = jnp.sum(jnp.where(lane == own, deg_lanes, 0.0), axis=1, keepdims=True)
    scale = lax.rsqrt(jnp.maximum(degree, 1.0))
    agg = (sums * scale).astype(BF16)
    pre = jnp.dot(agg, weight_ref[...], preferred_element_type=F32) + bias_ref[...]
    sigma = jax.nn.sigmoid(pre)
    out_ref[...] = (pre * sigma).astype(BF16)
    grad = (cot_ref[...].astype(F32) * (sigma * (1.0 + pre * (1.0 - sigma)))).astype(BF16)
    dsum = (dot_nt(grad, weight_ref[...]) * scale).astype(BF16)
    weight_term = lax.dot_general(agg, grad, TN, preferred_element_type=F32)
    bias_rows = bias_block(jnp.sum(grad.astype(F32), axis=0, keepdims=True))
    weight_term = weight_term.astype(BF16)
    for j in range(n_col):
        chunk = weight_term[16 * j : 16 * (j + 1), :]
        send_ref[j, :rows, :] = dsum[:, :LANES]
        send_ref[j, rows : 2 * rows, :] = dsum[:, LANES:]
        send_ref[j, 2 * rows : 2 * rows + 16, :] = chunk[:, :LANES]
        send_ref[j, 2 * rows + 16 : 2 * rows + 32, :] = chunk[:, LANES:]
        send_ref[j, 2 * rows + 32 :, :] = bias_rows


def backward_kernel(m_ref, recv_ref, send_ref, grads_ref):
    n_col, n_near = recv_ref.shape[0], send_ref.shape[0]
    size = m_ref.shape[0]
    rows, own = size // n_col, size // (n_near * FAR)
    extra = recv_ref[0, 2 * rows :, :].astype(F32)
    for j in range(1, n_col):
        extra += recv_ref[j, 2 * rows :, :].astype(F32)
    chunk = extra[:32, :].astype(BF16)
    bias_rows = merged_bias(extra[32:, :])
    for j in range(n_col):
        grads_ref[j * rows : (j + 1) * rows, :LANES] = recv_ref[j, :rows, :]
        grads_ref[j * rows : (j + 1) * rows, LANES:] = recv_ref[j, rows : 2 * rows, :]
    for i in range(n_near):
        part = m_ref[:, i * FAR * own : (i + 1) * FAR * own]
        sums = lax.dot_general(part, grads_ref[...], TN, preferred_element_type=F32).astype(BF16)
        for k in range(FAR):
            base = 2 * own * k
            send_ref[i, base : base + own, :] = sums[k * own : (k + 1) * own, :LANES]
            send_ref[i, base + own : base + 2 * own, :] = sums[k * own : (k + 1) * own, LANES:]
        send_ref[i, 2 * own * FAR : 2 * own * FAR + 32, :] = chunk
        send_ref[i, 2 * own * FAR + 32 :, :] = bias_rows


def merged_bias(rows):
    bias = rows[:2, :] + rows[2:4, :]
    return bias_block(jnp.concatenate([bias[:1, :], bias[1:, :]], axis=1))


def middle_kernel(recv_ref, send_ref):
    part = (recv_ref.shape[1] - 40) // FAR
    total = recv_ref[0].astype(F32)
    for i in range(1, recv_ref.shape[0]):
        total += recv_ref[i].astype(F32)
    base = part * FAR
    chunk = total[base : base + 32, :].astype(BF16)
    bias_rows = merged_bias(total[base + 32 :, :])
    for k in range(FAR):
        send_ref[k, :part, :] = total[k * part : (k + 1) * part, :].astype(BF16)
        send_ref[k, part : part + 32, :] = chunk
        send_ref[k, part + 32 :, :] = bias_rows


def final_kernel(recv_ref, feature_ref, bias_ref, spread_ref):
    own = feature_ref.shape[0]
    total = recv_ref[0].astype(F32)
    for i in range(1, recv_ref.shape[0]):
        total += recv_ref[i].astype(F32)
    feature_ref[:, :LANES] = total[:own, :].astype(BF16)
    feature_ref[:, LANES:] = total[own : 2 * own, :].astype(BF16)
    base = 2 * own
    for i in range(spread_ref.shape[0]):
        spread_ref[i, :, :LANES] = total[base : base + 16, :]
        spread_ref[i, :, LANES:] = total[base + 16 : base + 32, :]
    bias = total[base + 32 : base + 34, :] + total[base + 34 : base + 36, :]
    bias_ref[:, :LANES] = bias[:1, :]
    bias_ref[:, LANES:] = bias[1:, :]


def exchange(blocks, axes):
    return lax.all_to_all(blocks, axes, split_axis=0, concat_axis=0, tiled=True)


def call(kernel, out_shape, in_specs, scratch=(), vmem=8, **options):
    several = isinstance(out_shape, tuple)
    return pl.pallas_call(
        kernel,
        out_shape=out_shape,
        in_specs=in_specs,
        out_specs=(VMEM,) * len(out_shape) if several else VMEM,
        scratch_shapes=list(scratch),
        compiler_params=pltpu.CompilerParams(vmem_limit_bytes=vmem * 2**20),
        name=kernel.__name__,
        **options,
    )


def make_body(n_row, n_col):
    near_axes = ("half", "near")
    n_near = HALVES * NEAR

    def body(
        features,
        node_order,
        tile_weights,
        tile_rows,
        tile_cols,
        tile_count,
        weight,
        bias_vector,
        cotangent,
    ):
        own, width = features.shape[1], features.shape[2]
        size = n_row * own
        rows = cotangent.shape[0]
        shape = jax.ShapeDtypeStruct
        sends = call(spread_kernel, shape((FAR, own, width), BF16), [VMEM])(features)
        some = exchange(sends, "far")
        matrix, degree = call(
            edges_kernel,
            (shape((size, size), BF16), shape((8, n_col * LANES), BF16)),
            [SMEM, SMEM, SMEM, VMEM, VMEM],
            [pltpu.VMEM((size, size), BF16), pltpu.VMEM((size, size), BF16)],
            vmem=12,
            cost_estimate=pl.CostEstimate(flops=4 * size**3, bytes_accessed=3 * 2**20, transcendentals=0),
        )(tile_count, tile_rows, tile_cols, node_order, tile_weights)
        sends = call(spread_kernel, shape((n_near, FAR * own, width), BF16), [VMEM])(some)
        gathered = exchange(sends, near_axes).reshape(size, width)
        send_sums = call(forward_kernel, shape((n_col, 2 * rows + 8, LANES), BF16), [VMEM] * 3)(
            matrix, gathered, degree
        )
        recv_sums = exchange(send_sums, "col")
        output, send_grads = call(
            dense_kernel,
            (shape((rows, width), BF16), shape((n_col, 2 * rows + 40, LANES), BF16)),
            [VMEM] * 4,
        )(recv_sums, weight, bias_vector.reshape(1, width), cotangent)
        recv_grads = exchange(send_grads, "col")
        send_back = call(
            backward_kernel,
            shape((n_near, 2 * own * FAR + 40, LANES), BF16),
            [VMEM] * 2,
            [pltpu.VMEM((size, width), BF16)],
        )(matrix, recv_grads)
        recv_near = exchange(send_back, near_axes)
        send_far = call(middle_kernel, shape((FAR, 2 * own + 40, LANES), BF16), [VMEM])(recv_near)
        recv_back = exchange(send_far, "far")
        feature_grad, bias_grad, send_weight = call(
            final_kernel,
            (
                shape((own, width), BF16),
                shape((1, width), F32),
                shape((n_col, 16, width), F32),
            ),
            [VMEM],
        )(recv_back)
        weight_grad = exchange(send_weight, "col").reshape(width, width)
        return (output, feature_grad[None], weight_grad, bias_grad.reshape(width))

    return body


def solution(mesh):
    n_row, n_col = mesh.shape["row"], mesh.shape["col"]
    row = ("half", "far", "near")
    split = Mesh(mesh.devices.reshape(HALVES, FAR, NEAR, n_col), row + ("col",))
    return jax.shard_map(
        make_body(n_row, n_col),
        mesh=split,
        in_specs=(
            P("col", row, None),
            P("col", None),
            P(row + ("col",), None, None),
            P(row + ("col",)),
            P(row + ("col",)),
            P(row + ("col",)),
            P(),
            P(),
            P(row + ("col",), None),
        ),
        out_specs=(P(row + ("col",), None), P("col", row, None), P(), P()),
        check_vma=False,
    )
```

```python
import jax
import jax.numpy as jnp
from jax import lax
from jax.experimental import pallas as pl
from jax.experimental.pallas import tpu as pltpu
from jax.sharding import Mesh, PartitionSpec as P

BF16 = jnp.bfloat16
F32 = jnp.float32
LANES = 128
HALVES, FAR, NEAR = 2, 8, 2
NT = (((1,), (1,)), ((), ()))
TN = (((0,), (0,)), ((), ()))
VMEM = pl.BlockSpec(memory_space=pltpu.VMEM)
SMEM = pl.BlockSpec(memory_space=pltpu.SMEM)


def dot_nt(left, right):
    return lax.dot_general(left, right, NT, preferred_element_type=F32)


def rows_block(rows, height=8):
    index = lax.broadcasted_iota(jnp.int32, (height, LANES), 0)
    block = jnp.zeros((height, LANES), F32)
    for k, row in enumerate(rows):
        block = jnp.where(index == k, row, block)
    return block


def bias_block(row):
    high = row.astype(BF16).astype(F32)
    low = row - high
    return rows_block([high[:, :LANES], high[:, LANES:], low[:, :LANES], low[:, LANES:]]).astype(BF16)


def spread_kernel(block_ref, out_ref):
    for i in range(out_ref.shape[0]):
        out_ref[i] = block_ref[...].reshape(out_ref.shape[1:])


def exchanged_place(place, own):
    low, block = place & (own - 1), place >> (own.bit_length() - 1)
    near, block = block & (NEAR - 1), block >> (NEAR.bit_length() - 1)
    far, half = block & (FAR - 1), block >> (FAR.bit_length() - 1)
    return ((half * NEAR + near) * FAR + far) * own + low


def edges_kernel(count_ref, rows_ref, cols_ref, order_ref, tiles_ref, m_ref, deg_ref, a_ref, p_ref):
    a_ref[...] = jnp.zeros_like(a_ref)
    tile = tiles_ref.shape[1]

    def add_slot(slot, carry):
        row = pl.multiple_of(rows_ref[slot] * tile, tile)
        col = pl.multiple_of(cols_ref[slot] * tile, tile)
        a_ref[pl.ds(row, tile), pl.ds(col, tile)] += tiles_ref[slot]
        return carry

    lax.fori_loop(0, count_ref[0], add_slot, 0)
    size = a_ref.shape[0]
    own = size // (HALVES * FAR * NEAR)
    order = jnp.broadcast_to(exchanged_place(order_ref[...], own), (size, size))
    places = lax.broadcasted_iota(jnp.int32, (size, size), 0)
    p_ref[...] = jnp.where(places == order, 1.0, 0.0).astype(BF16)
    step = 256
    for start in range(0, size, step):
        part = slice(start, start + step)
        m_ref[:, part] = dot_nt(a_ref[...], p_ref[part, :]).astype(BF16)
    degree = dot_nt(jnp.ones((16, size), BF16), a_ref[...])[:8, :]
    high = jnp.floor(degree * (1.0 / 128.0))
    index = lax.broadcasted_iota(jnp.int32, degree.shape, 0)
    pairs = jnp.where(index == 0, high, degree - 128.0 * high)
    rows = size * LANES // deg_ref.shape[1]
    for j in range(size // rows):
        block = pairs[:, j * rows // LANES * LANES :][:, :LANES]
        first = j * rows % LANES
        if first:
            block = jnp.concatenate([block[:, first:], block[:, :first]], axis=1)
        deg_ref[:, j * LANES : (j + 1) * LANES] = block.astype(BF16)


def forward_kernel(m_ref, features_ref, deg_ref, send_ref):
    n_col = send_ref.shape[0]
    rows = m_ref.shape[0] // n_col
    group = 4
    for start in range(0, n_col, group):
        sums = jnp.dot(
            m_ref[start * rows : (start + group) * rows, :], features_ref[...], preferred_element_type=F32
        ).astype(BF16)
        for k in range(group):
            send_ref[start + k, :rows, :] = sums[k * rows : (k + 1) * rows, :LANES]
            send_ref[start + k, rows : 2 * rows, :] = sums[k * rows : (k + 1) * rows, LANES:]
    for j in range(n_col):
        send_ref[j, 2 * rows :, :] = deg_ref[:, j * LANES : (j + 1) * LANES]


def dense_kernel(recv_ref, weight_ref, bias_ref, cot_ref, out_ref, send_ref):
    n_col, rows = recv_ref.shape[0], cot_ref.shape[0]
    total = recv_ref[0].astype(F32)
    for j in range(1, n_col):
        total += recv_ref[j].astype(F32)
    sums = jnp.concatenate([total[:rows, :], total[rows : 2 * rows, :]], axis=1)
    deg_lanes = 128.0 * total[2 * rows : 2 * rows + 1, :] + total[2 * rows + 1 : 2 * rows + 2, :]
    lane = lax.broadcasted_iota(jnp.int32, (rows, LANES), 1)
    own = lax.broadcasted_iota(jnp.int32, (rows, LANES), 0)
    degree = jnp.sum(jnp.where(lane == own, deg_lanes, 0.0), axis=1, keepdims=True)
    scale = lax.rsqrt(jnp.maximum(degree, 1.0))
    agg = (sums * scale).astype(BF16)
    pre = jnp.dot(agg, weight_ref[...], preferred_element_type=F32) + bias_ref[...]
    sigma = jax.nn.sigmoid(pre)
    out_ref[...] = (pre * sigma).astype(BF16)
    grad = (cot_ref[...].astype(F32) * (sigma * (1.0 + pre * (1.0 - sigma)))).astype(BF16)
    dsum = (dot_nt(grad, weight_ref[...]) * scale).astype(BF16)
    weight_term = lax.dot_general(agg, grad, TN, preferred_element_type=F32)
    bias_rows = bias_block(jnp.sum(grad.astype(F32), axis=0, keepdims=True))
    weight_term = weight_term.astype(BF16)
    for j in range(n_col):
        chunk = weight_term[16 * j : 16 * (j + 1), :]
        send_ref[j, :rows, :] = dsum[:, :LANES]
        send_ref[j, rows : 2 * rows, :] = dsum[:, LANES:]
        send_ref[j, 2 * rows : 2 * rows + 16, :] = chunk[:, :LANES]
        send_ref[j, 2 * rows + 16 : 2 * rows + 32, :] = chunk[:, LANES:]
        send_ref[j, 2 * rows + 32 :, :] = bias_rows


def backward_kernel(m_ref, recv_ref, send_ref, grads_ref):
    n_col, n_near = recv_ref.shape[0], send_ref.shape[0]
    size = m_ref.shape[0]
    rows, own = size // n_col, size // (n_near * FAR)
    extra = recv_ref[0, 2 * rows :, :].astype(F32)
    for j in range(1, n_col):
        extra += recv_ref[j, 2 * rows :, :].astype(F32)
    chunk = extra[:32, :].astype(BF16)
    bias_rows = merged_bias(extra[32:, :])
    for j in range(n_col):
        grads_ref[j * rows : (j + 1) * rows, :LANES] = recv_ref[j, :rows, :]
        grads_ref[j * rows : (j + 1) * rows, LANES:] = recv_ref[j, rows : 2 * rows, :]
    for i in range(n_near):
        part = m_ref[:, i * FAR * own : (i + 1) * FAR * own]
        sums = lax.dot_general(part, grads_ref[...], TN, preferred_element_type=F32).astype(BF16)
        for k in range(FAR):
            base = 2 * own * k
            send_ref[i, base : base + own, :] = sums[k * own : (k + 1) * own, :LANES]
            send_ref[i, base + own : base + 2 * own, :] = sums[k * own : (k + 1) * own, LANES:]
        send_ref[i, 2 * own * FAR : 2 * own * FAR + 32, :] = chunk
        send_ref[i, 2 * own * FAR + 32 :, :] = bias_rows


def merged_bias(rows):
    bias = rows[:2, :] + rows[2:4, :]
    return bias_block(jnp.concatenate([bias[:1, :], bias[1:, :]], axis=1))


def middle_kernel(recv_ref, send_ref):
    part = (recv_ref.shape[1] - 40) // FAR
    total = recv_ref[0].astype(F32)
    for i in range(1, recv_ref.shape[0]):
        total += recv_ref[i].astype(F32)
    base = part * FAR
    chunk = total[base : base + 32, :].astype(BF16)
    bias_rows = merged_bias(total[base + 32 :, :])
    for k in range(FAR):
        send_ref[k, :part, :] = total[k * part : (k + 1) * part, :].astype(BF16)
        send_ref[k, part : part + 32, :] = chunk
        send_ref[k, part + 32 :, :] = bias_rows


def weight_kernel(recv_ref, spread_ref):
    base = recv_ref.shape[1] - 40
    total = recv_ref[0, base : base + 32, :].astype(F32)
    for i in range(1, recv_ref.shape[0]):
        total += recv_ref[i, base : base + 32, :].astype(F32)
    for i in range(spread_ref.shape[0]):
        spread_ref[i, :, :LANES] = total[:16, :]
        spread_ref[i, :, LANES:] = total[16:, :]


def store_kernel(recv_ref, chunks_ref, output_ref, feature_ref, bias_ref, weight_ref, out_ref):
    own = feature_ref.shape[0]
    total = recv_ref[0].astype(F32)
    for i in range(1, recv_ref.shape[0]):
        total += recv_ref[i].astype(F32)
    feature_ref[:, :LANES] = total[:own, :].astype(BF16)
    feature_ref[:, LANES:] = total[own : 2 * own, :].astype(BF16)
    base = 2 * own + 32
    bias = total[base : base + 2, :] + total[base + 2 : base + 4, :]
    bias_ref[:, :LANES] = bias[:1, :]
    bias_ref[:, LANES:] = bias[1:, :]
    weight_ref[...] = chunks_ref[...].reshape(weight_ref.shape)
    out_ref[...] = output_ref[...]


def exchange(blocks, axes):
    return lax.all_to_all(blocks, axes, split_axis=0, concat_axis=0, tiled=True)


def call(kernel, out_shape, in_specs, scratch=(), vmem=8, **options):
    several = isinstance(out_shape, tuple)
    return pl.pallas_call(
        kernel,
        out_shape=out_shape,
        in_specs=in_specs,
        out_specs=(VMEM,) * len(out_shape) if several else VMEM,
        scratch_shapes=list(scratch),
        compiler_params=pltpu.CompilerParams(vmem_limit_bytes=vmem * 2**20),
        name=kernel.__name__,
        **options,
    )


def make_body(n_row, n_col):
    near_axes = ("half", "near")
    n_near = HALVES * NEAR

    def body(
        features,
        node_order,
        tile_weights,
        tile_rows,
        tile_cols,
        tile_count,
        weight,
        bias_vector,
        cotangent,
    ):
        own, width = features.shape[1], features.shape[2]
        size = n_row * own
        rows = cotangent.shape[0]
        shape = jax.ShapeDtypeStruct
        sends = call(spread_kernel, shape((FAR, own, width), BF16), [VMEM])(features)
        some = exchange(sends, "far")
        matrix, degree = call(
            edges_kernel,
            (shape((size, size), BF16), shape((8, n_col * LANES), BF16)),
            [SMEM, SMEM, SMEM, VMEM, VMEM],
            [pltpu.VMEM((size, size), BF16), pltpu.VMEM((size, size), BF16)],
            vmem=12,
            cost_estimate=pl.CostEstimate(flops=4 * size**3, bytes_accessed=3 * 2**20, transcendentals=0),
        )(tile_count, tile_rows, tile_cols, node_order, tile_weights)
        sends = call(spread_kernel, shape((n_near, FAR * own, width), BF16), [VMEM])(some)
        gathered = exchange(sends, near_axes).reshape(size, width)
        send_sums = call(forward_kernel, shape((n_col, 2 * rows + 8, LANES), BF16), [VMEM] * 3)(
            matrix, gathered, degree
        )
        recv_sums = exchange(send_sums, "col")
        output, send_grads = call(
            dense_kernel,
            (shape((rows, width), BF16), shape((n_col, 2 * rows + 40, LANES), BF16)),
            [VMEM] * 4,
        )(recv_sums, weight, bias_vector.reshape(1, width), cotangent)
        recv_grads = exchange(send_grads, "col")
        send_back = call(
            backward_kernel,
            shape((n_near, 2 * own * FAR + 40, LANES), BF16),
            [VMEM] * 2,
            [pltpu.VMEM((size, width), BF16)],
        )(matrix, recv_grads)
        recv_near = exchange(send_back, near_axes)
        send_far = call(middle_kernel, shape((FAR, 2 * own + 40, LANES), BF16), [VMEM])(recv_near)
        recv_back = exchange(send_far, "far")
        send_weight = call(weight_kernel, shape((n_col, 16, width), F32), [VMEM])(recv_back)
        chunks = exchange(send_weight, "col")
        feature_grad, bias_grad, weight_grad, output = call(
            store_kernel,
            (
                shape((own, width), BF16),
                shape((1, width), F32),
                shape((width, width), F32),
                shape((rows, width), BF16),
            ),
            [VMEM] * 3,
        )(recv_back, chunks, output)
        return (output, feature_grad[None], weight_grad, bias_grad.reshape(width))

    return body


def solution(mesh):
    n_row, n_col = mesh.shape["row"], mesh.shape["col"]
    row = ("half", "far", "near")
    split = Mesh(mesh.devices.reshape(HALVES, FAR, NEAR, n_col), row + ("col",))
    return jax.shard_map(
        make_body(n_row, n_col),
        mesh=split,
        in_specs=(
            P("col", row, None),
            P("col", None),
            P(row + ("col",), None, None),
            P(row + ("col",)),
            P(row + ("col",)),
            P(row + ("col",)),
            P(),
            P(),
            P(row + ("col",), None),
        ),
        out_specs=(P(row + ("col",), None), P("col", row, None), P(), P()),
        check_vma=False,
    )
```

```python
import jax
import jax.numpy as jnp
from jax import lax
from jax.experimental import pallas as pl
from jax.experimental.pallas import tpu as pltpu
from jax.sharding import Mesh, PartitionSpec as P

BF16 = jnp.bfloat16
F32 = jnp.float32
LANES = 128
HALVES, FAR, NEAR = 2, 8, 2
NT = (((1,), (1,)), ((), ()))
TN = (((0,), (0,)), ((), ()))
VMEM = pl.BlockSpec(memory_space=pltpu.VMEM)
SMEM = pl.BlockSpec(memory_space=pltpu.SMEM)


def dot_nt(left, right):
    return lax.dot_general(left, right, NT, preferred_element_type=F32)


def rows_block(rows, height=8):
    index = lax.broadcasted_iota(jnp.int32, (height, LANES), 0)
    block = jnp.zeros((height, LANES), F32)
    for k, row in enumerate(rows):
        block = jnp.where(index == k, row, block)
    return block


def bias_block(row):
    high = row.astype(BF16).astype(F32)
    low = row - high
    return rows_block([high[:, :LANES], high[:, LANES:], low[:, :LANES], low[:, LANES:]]).astype(BF16)


def spread_kernel(block_ref, out_ref):
    for i in range(out_ref.shape[0]):
        out_ref[i] = block_ref[...].reshape(out_ref.shape[1:])


def exchanged_place(place, own):
    low, block = place & (own - 1), place >> (own.bit_length() - 1)
    near, block = block & (NEAR - 1), block >> (NEAR.bit_length() - 1)
    far, half = block & (FAR - 1), block >> (FAR.bit_length() - 1)
    return ((half * NEAR + near) * FAR + far) * own + low


def edges_kernel(count_ref, rows_ref, cols_ref, order_ref, tiles_ref, m_ref, deg_ref, a_ref, p_ref):
    a_ref[...] = jnp.zeros_like(a_ref)
    tile = tiles_ref.shape[1]

    def add_slot(slot, carry):
        row = pl.multiple_of(rows_ref[slot] * tile, tile)
        col = pl.multiple_of(cols_ref[slot] * tile, tile)
        a_ref[pl.ds(row, tile), pl.ds(col, tile)] += tiles_ref[slot]
        return carry

    lax.fori_loop(0, count_ref[0], add_slot, 0)
    size = a_ref.shape[0]
    own = size // (HALVES * FAR * NEAR)
    order = jnp.broadcast_to(exchanged_place(order_ref[...], own), (size, size))
    places = lax.broadcasted_iota(jnp.int32, (size, size), 0)
    p_ref[...] = jnp.where(places == order, 1.0, 0.0).astype(BF16)
    step = 256
    for start in range(0, size, step):
        part = slice(start, start + step)
        m_ref[:, part] = dot_nt(a_ref[...], p_ref[part, :]).astype(BF16)
    degree = dot_nt(jnp.ones((16, size), BF16), a_ref[...])[:8, :]
    high = jnp.floor(degree * (1.0 / 128.0))
    index = lax.broadcasted_iota(jnp.int32, degree.shape, 0)
    pairs = jnp.where(index == 0, high, degree - 128.0 * high)
    rows = size * LANES // deg_ref.shape[1]
    for j in range(size // rows):
        block = pairs[:, j * rows // LANES * LANES :][:, :LANES]
        first = j * rows % LANES
        if first:
            block = jnp.concatenate([block[:, first:], block[:, :first]], axis=1)
        deg_ref[:, j * LANES : (j + 1) * LANES] = block.astype(BF16)


def forward_kernel(m_ref, features_ref, deg_ref, send_ref):
    n_col = send_ref.shape[0]
    rows = m_ref.shape[0] // n_col
    group = 4
    for start in range(0, n_col, group):
        sums = jnp.dot(
            m_ref[start * rows : (start + group) * rows, :], features_ref[...], preferred_element_type=F32
        ).astype(BF16)
        for k in range(group):
            send_ref[start + k, :rows, :] = sums[k * rows : (k + 1) * rows, :LANES]
            send_ref[start + k, rows : 2 * rows, :] = sums[k * rows : (k + 1) * rows, LANES:]
    for j in range(n_col):
        send_ref[j, 2 * rows :, :] = deg_ref[:, j * LANES : (j + 1) * LANES]


def dense_kernel(recv_ref, weight_ref, bias_ref, cot_ref, out_ref, send_ref):
    n_col, rows = recv_ref.shape[0], cot_ref.shape[0]
    total = recv_ref[0].astype(F32)
    for j in range(1, n_col):
        total += recv_ref[j].astype(F32)
    sums = jnp.concatenate([total[:rows, :], total[rows : 2 * rows, :]], axis=1)
    deg_lanes = 128.0 * total[2 * rows : 2 * rows + 1, :] + total[2 * rows + 1 : 2 * rows + 2, :]
    lane = lax.broadcasted_iota(jnp.int32, (rows, LANES), 1)
    own = lax.broadcasted_iota(jnp.int32, (rows, LANES), 0)
    degree = jnp.sum(jnp.where(lane == own, deg_lanes, 0.0), axis=1, keepdims=True)
    scale = lax.rsqrt(jnp.maximum(degree, 1.0))
    agg = (sums * scale).astype(BF16)
    pre = jnp.dot(agg, weight_ref[...], preferred_element_type=F32) + bias_ref[...]
    sigma = jax.nn.sigmoid(pre)
    out_ref[...] = (pre * sigma).astype(BF16)
    grad = (cot_ref[...].astype(F32) * (sigma * (1.0 + pre * (1.0 - sigma)))).astype(BF16)
    dsum = (dot_nt(grad, weight_ref[...]) * scale).astype(BF16)
    weight_term = lax.dot_general(agg, grad, TN, preferred_element_type=F32)
    bias_rows = bias_block(jnp.sum(grad.astype(F32), axis=0, keepdims=True))
    for j in range(n_col):
        chunk = jnp.concatenate(
            [weight_term[8 * (h * n_col + j) : 8 * (h * n_col + j + 1), :] for h in range(HALVES)], axis=0
        ).astype(BF16)
        send_ref[j, :rows, :] = dsum[:, :LANES]
        send_ref[j, rows : 2 * rows, :] = dsum[:, LANES:]
        send_ref[j, 2 * rows : 2 * rows + 16, :] = chunk[:, :LANES]
        send_ref[j, 2 * rows + 16 : 2 * rows + 32, :] = chunk[:, LANES:]
        send_ref[j, 2 * rows + 32 :, :] = bias_rows


def backward_kernel(m_ref, recv_ref, send_ref, grads_ref):
    n_col, n_near = recv_ref.shape[0], send_ref.shape[0]
    size = m_ref.shape[0]
    rows, own = size // n_col, size // (n_near * FAR)
    extra = recv_ref[0, 2 * rows :, :].astype(F32)
    for j in range(1, n_col):
        extra += recv_ref[j, 2 * rows :, :].astype(F32)
    chunks = [
        jnp.concatenate([extra[8 * h : 8 * h + 8, :], extra[16 + 8 * h : 24 + 8 * h, :]], axis=0).astype(BF16)
        for h in range(HALVES)
    ]
    bias_rows = merged_bias(extra[32:, :])
    for j in range(n_col):
        grads_ref[j * rows : (j + 1) * rows, :LANES] = recv_ref[j, :rows, :]
        grads_ref[j * rows : (j + 1) * rows, LANES:] = recv_ref[j, rows : 2 * rows, :]
    for i in range(n_near):
        part = m_ref[:, i * FAR * own : (i + 1) * FAR * own]
        sums = lax.dot_general(part, grads_ref[...], TN, preferred_element_type=F32).astype(BF16)
        for k in range(FAR):
            base = 2 * own * k
            send_ref[i, base : base + own, :] = sums[k * own : (k + 1) * own, :LANES]
            send_ref[i, base + own : base + 2 * own, :] = sums[k * own : (k + 1) * own, LANES:]
        send_ref[i, 2 * own * FAR : 2 * own * FAR + 16, :] = chunks[i // NEAR]
        send_ref[i, 2 * own * FAR + 16 :, :] = bias_rows


def merged_bias(rows):
    bias = rows[:2, :] + rows[2:4, :]
    return bias_block(jnp.concatenate([bias[:1, :], bias[1:, :]], axis=1))


def middle_kernel(recv_ref, send_ref):
    part = (recv_ref.shape[1] - 24) // FAR
    total = recv_ref[0].astype(F32)
    for i in range(1, recv_ref.shape[0]):
        total += recv_ref[i].astype(F32)
    base = part * FAR
    chunk = total[base : base + 16, :].astype(BF16)
    bias_rows = merged_bias(total[base + 16 :, :])
    for k in range(FAR):
        send_ref[k, :part, :] = total[k * part : (k + 1) * part, :].astype(BF16)
        send_ref[k, part : part + 16, :] = chunk
        send_ref[k, part + 16 :, :] = bias_rows


def weight_kernel(recv_ref, spread_ref):
    base = recv_ref.shape[1] - 24
    total = recv_ref[0, base : base + 16, :].astype(F32)
    for i in range(1, recv_ref.shape[0]):
        total += recv_ref[i, base : base + 16, :].astype(F32)
    for i in range(spread_ref.shape[0]):
        spread_ref[i, :, :LANES] = total[:8, :]
        spread_ref[i, :, LANES:] = total[8:, :]


def store_kernel(recv_ref, chunks_ref, output_ref, feature_ref, bias_ref, weight_ref, out_ref):
    own = feature_ref.shape[0]
    total = recv_ref[0].astype(F32)
    for i in range(1, recv_ref.shape[0]):
        total += recv_ref[i].astype(F32)
    feature_ref[:, :LANES] = total[:own, :].astype(BF16)
    feature_ref[:, LANES:] = total[own : 2 * own, :].astype(BF16)
    base = 2 * own + 16
    bias = total[base : base + 2, :] + total[base + 2 : base + 4, :]
    bias_ref[:, :LANES] = bias[:1, :]
    bias_ref[:, LANES:] = bias[1:, :]
    weight_ref[...] = chunks_ref[...].reshape(weight_ref.shape)
    out_ref[...] = output_ref[...]


def exchange(blocks, axes):
    return lax.all_to_all(blocks, axes, split_axis=0, concat_axis=0, tiled=True)


def call(kernel, out_shape, in_specs, scratch=(), vmem=8, **options):
    several = isinstance(out_shape, tuple)
    return pl.pallas_call(
        kernel,
        out_shape=out_shape,
        in_specs=in_specs,
        out_specs=(VMEM,) * len(out_shape) if several else VMEM,
        scratch_shapes=list(scratch),
        compiler_params=pltpu.CompilerParams(vmem_limit_bytes=vmem * 2**20),
        name=kernel.__name__,
        **options,
    )


def make_body(n_row, n_col):
    near_axes = ("half", "near")
    n_near = HALVES * NEAR

    def body(
        features,
        node_order,
        tile_weights,
        tile_rows,
        tile_cols,
        tile_count,
        weight,
        bias_vector,
        cotangent,
    ):
        own, width = features.shape[1], features.shape[2]
        size = n_row * own
        rows = cotangent.shape[0]
        shape = jax.ShapeDtypeStruct
        sends = call(spread_kernel, shape((FAR, own, width), BF16), [VMEM])(features)
        some = exchange(sends, "far")
        matrix, degree = call(
            edges_kernel,
            (shape((size, size), BF16), shape((8, n_col * LANES), BF16)),
            [SMEM, SMEM, SMEM, VMEM, VMEM],
            [pltpu.VMEM((size, size), BF16), pltpu.VMEM((size, size), BF16)],
            vmem=12,
            cost_estimate=pl.CostEstimate(flops=4 * size**3, bytes_accessed=3 * 2**20, transcendentals=0),
        )(tile_count, tile_rows, tile_cols, node_order, tile_weights)
        sends = call(spread_kernel, shape((n_near, FAR * own, width), BF16), [VMEM])(some)
        gathered = exchange(sends, near_axes).reshape(size, width)
        send_sums = call(forward_kernel, shape((n_col, 2 * rows + 8, LANES), BF16), [VMEM] * 3)(
            matrix, gathered, degree
        )
        recv_sums = exchange(send_sums, "col")
        output, send_grads = call(
            dense_kernel,
            (shape((rows, width), BF16), shape((n_col, 2 * rows + 40, LANES), BF16)),
            [VMEM] * 4,
        )(recv_sums, weight, bias_vector.reshape(1, width), cotangent)
        recv_grads = exchange(send_grads, "col")
        send_back = call(
            backward_kernel,
            shape((n_near, 2 * own * FAR + 24, LANES), BF16),
            [VMEM] * 2,
            [pltpu.VMEM((size, width), BF16)],
        )(matrix, recv_grads)
        recv_near = exchange(send_back, near_axes)
        send_far = call(middle_kernel, shape((FAR, 2 * own + 24, LANES), BF16), [VMEM])(recv_near)
        recv_back = exchange(send_far, "far")
        send_weight = call(weight_kernel, shape((HALVES * n_col, 8, width), F32), [VMEM])(recv_back)
        chunks = exchange(send_weight, ("half", "col"))
        feature_grad, bias_grad, weight_grad, output = call(
            store_kernel,
            (
                shape((own, width), BF16),
                shape((1, width), F32),
                shape((width, width), F32),
                shape((rows, width), BF16),
            ),
            [VMEM] * 3,
        )(recv_back, chunks, output)
        return (output, feature_grad[None], weight_grad, bias_grad.reshape(width))

    return body


def solution(mesh):
    n_row, n_col = mesh.shape["row"], mesh.shape["col"]
    row = ("half", "far", "near")
    split = Mesh(mesh.devices.reshape(HALVES, FAR, NEAR, n_col), row + ("col",))
    return jax.shard_map(
        make_body(n_row, n_col),
        mesh=split,
        in_specs=(
            P("col", row, None),
            P("col", None),
            P(row + ("col",), None, None),
            P(row + ("col",)),
            P(row + ("col",)),
            P(row + ("col",)),
            P(),
            P(),
            P(row + ("col",), None),
        ),
        out_specs=(P(row + ("col",), None), P("col", row, None), P(), P()),
        check_vma=False,
    )
```
